256 devices in a mesh: cube: 8 (over z), front: 32 (over x, y, core).
Axes of the slice: x: 4, y: 4, z: 8, core: 2. Of those that a mesh axis runs over, the one named last changes fastest.
Arguments:
- right_sides: float32 [3, 8, 2048, 128], P(None, 'cube', 'front'), may hold values from -6 to 6
- inverse_leaf: float32 [8, 2048, 2048], P('cube', 'front'), may hold values from -2 to 2, as said below
- inverse_mid: float32 [8, 2048, 4096], P('cube', 'front'), may hold values from -2 to 2, as said below
- inverse_top: float32 [8, 2048, 8192], P('cube', 'front'), may hold values from -2 to 2, as said below
- coupling_mid: float32 [8, 2048, 4096], P('cube', 'front'), may hold values from -0.1875 to 0.1875
- coupling_top: float32 [8, 2048, 8192], P('cube', 'front'), may hold values from -0.125 to 0.125
- pattern_mid: int32 [8, 32, 64], P('cube', 'front'), may hold values 0 or 1
- pattern_top: int32 [8, 32, 128], P('cube', 'front'), may hold values 0 or 1
Outputs:
- solution: float32 [3, 8, 2048, 128], P(None, 'cube', 'front')
The draws below stay inside these ranges and needn't reach their ends.
Inputs may be any that keep to these rules, and one draw needn't show every extreme that they name: `inverse_leaf`: each block is the inverse of a lower triangular diagonal block: zero above the diagonal of the separator's row order, diagonal 1 to 2. `inverse_mid`: as inverse_leaf. `inverse_top`: as inverse_leaf.
All inputs are finite; a program needn't handle non-finite values. No bound on the sum of `pattern_mid` or of `pattern_top` on one device may be relied on, other than what follows from the above.
Results may differ from the reference program's by a relative error of at most 0.00013.
Values sent between devices are 32-bit elements; how exact they have to be, the bound alone decides.
A program may use at most 64 MiB of HBM per device.

```python
import jax
import jax.numpy as jnp
from jax import lax

TILE = 64
NRHS = 128
LEVELS = 3
SEP = 2048
N_CUBE = 8


def lower_block(key, members):
    width = members * SEP
    key_noise, key_diag = jax.random.split(key, 2)
    node_row = ((jnp.arange(N_CUBE) % members)[:, None] * SEP + jnp.arange(SEP)[None, :])[:, :, None]
    column = jnp.arange(width)[None, None, :]
    noise = jnp.clip(jax.random.normal(key_noise, (N_CUBE, SEP, width), jnp.float32), -6.0, 6.0)
    off_diag = noise * (0.5 / width ** 0.5)
    diagonal = 1.0 + jax.random.uniform(key_diag, (N_CUBE, SEP, 1), jnp.float32)
    lower = jnp.where(column < node_row, off_diag, 0.0)
    return lower + jnp.where(column == node_row, diagonal, 0.0)


def draw_inverse_leaf(key, part):
    return lower_block(jax.random.fold_in(key, 11), 1)


def draw_inverse_mid(key, part):
    return lower_block(jax.random.fold_in(key, 12), 2)


def draw_inverse_top(key, part):
    return lower_block(jax.random.fold_in(key, 13), 4)


def plant(drawn, rng, smallest, top_value):
    longest = drawn.shape.index(max(drawn.shape))
    spots = []
    for shift in (0, 1):
        where = [jax.random.randint(jax.random.fold_in(rng, axis), (), 0, length) for axis, length in enumerate(drawn.shape)]
        where[longest] = (where[longest] + shift) % drawn.shape[longest]
        spots.append(tuple(where))
    return drawn.at[spots[0]].set(smallest).at[spots[1]].set(top_value)


def raised(entries, own_key, source, target, blocks, factor):
    def block_of(dim):
        return (jnp.arange(entries.shape[dim]) // (entries.shape[dim] // blocks)).reshape((-1,) + (1,) * (entries.ndim - 1 - dim))

    one_side = jax.random.permutation(own_key, blocks)[block_of(target)]
    second = (block_of(target) + blocks // 2) % blocks
    return jnp.where((block_of(source) == one_side) | (block_of(source) == second), factor * entries, entries)


def block_scale(own_key, dims, cuts, low, largest):
    loudness = 1.0
    for position, parts in cuts:
        heights = jax.random.uniform(jax.random.fold_in(jax.random.fold_in(own_key, 6), position), (parts,), jnp.float32, low / len(cuts), largest / len(cuts))
        loudness = loudness * jnp.repeat(jnp.exp(heights), dims[position] // parts).reshape((-1,) + (1,) * (len(dims) - 1 - position))
    return loudness


def bell_draw(key, dims, scale, most, cuts=(), kind=jnp.bfloat16):
    level = block_scale(key, dims, cuts, -0.22, 0.18) if cuts else 1.0
    drawn = jax.random.normal(key, dims, jnp.float32) * scale * level
    return jnp.minimum(jnp.maximum(drawn, -most), most).astype(kind)


def noise_with(key, shape, scale, limit, pieces, heavy, dtype=jnp.bfloat16):
    result = scale * jax.random.normal(key, shape, jnp.float32)
    if pieces:
        result = result * block_scale(key, shape, pieces, -0.22, 0.18)
    return jnp.clip(raised(result, jax.random.fold_in(key, 3), *heavy), -limit, limit).astype(dtype)


def setup_inputs(seed: int = 0) -> dict:
    streams_of = jax.random.split(jax.random.key(seed), 9)
    return {
        "right_sides": bell_draw(streams_of[0], (LEVELS, N_CUBE, SEP, NRHS), 1.0, 6.0, ((1, 8), (2, 32)), jnp.float32),
        "inverse_leaf": draw_inverse_leaf(jax.random.fold_in(streams_of[8], 71), 0),
        "inverse_mid": draw_inverse_mid(jax.random.fold_in(streams_of[8], 71), 0),
        "inverse_top": draw_inverse_top(jax.random.fold_in(streams_of[8], 71), 0),
        "coupling_mid": noise_with(streams_of[4], (N_CUBE, SEP, 2 * SEP), (2 * SEP) ** -0.5, 0.1875, ((0, 8), (1, 32)), (1, 2, 32, 2.75), jnp.float32),
        "coupling_top": noise_with(streams_of[5], (N_CUBE, SEP, 4 * SEP), (4 * SEP) ** -0.5, 0.125, ((0, 8), (1, 32)), (1, 2, 32, 2.75), jnp.float32),
        "pattern_mid": plant((jax.random.randint(streams_of[6], (N_CUBE, SEP // TILE, 2 * SEP // TILE), 0, 4) < 3).astype(jnp.int32), jax.random.fold_in(streams_of[6], 1), 0, 1),
        "pattern_top": plant((jax.random.randint(streams_of[7], (N_CUBE, SEP // TILE, 4 * SEP // TILE), 0, 4) < 3).astype(jnp.int32), jax.random.fold_in(streams_of[7], 1), 0, 1),
    }


def masked(coupling, pattern):
    keep_rows = jnp.repeat(pattern, TILE, axis=1)
    keep_all = jnp.repeat(keep_rows, TILE, axis=2)
    return coupling * keep_all.astype(jnp.float32)


def grouped(array, members):
    return array.reshape(N_CUBE // members, members * array.shape[1], array.shape[2])


def flatten(array):
    return array.reshape(N_CUBE, SEP, array.shape[2])


def product(matrix, vector):
    return jnp.einsum("nij,njk->nik", matrix, vector, precision=lax.Precision.HIGHEST)


def transposed(matrix, vector):
    return jnp.einsum("nji,njk->nik", matrix, vector, precision=lax.Precision.HIGHEST)


def reference(right_sides, inverse_leaf, inverse_mid, inverse_top, coupling_mid, coupling_top, pattern_mid, pattern_top):
    block_mid = grouped(masked(coupling_mid, pattern_mid), 2)
    block_top = grouped(masked(coupling_top, pattern_top), 4)
    inv_leaf = grouped(inverse_leaf, 1)
    inv_mid = grouped(inverse_mid, 2)
    inv_top = grouped(inverse_top, 4)
    solved_leaf = product(inv_leaf, grouped(right_sides[0], 1))
    update_mid = product(block_mid, grouped(flatten(solved_leaf), 2))
    solved_mid = product(inv_mid, grouped(right_sides[1], 2) - update_mid)
    update_top = product(block_top, grouped(flatten(solved_mid), 4))
    solved_top = product(inv_top, grouped(right_sides[2], 4) - update_top)
    back_top = transposed(inv_top, solved_top)
    carry_mid = grouped(flatten(transposed(block_top, back_top)), 2)
    back_mid = transposed(inv_mid, solved_mid - carry_mid)
    carry_leaf = grouped(flatten(transposed(block_mid, back_mid)), 1)
    back_leaf = transposed(inv_leaf, solved_leaf - carry_leaf)
    return jnp.stack([flatten(back_leaf), flatten(back_mid), flatten(back_top)])
```

```python
import functools

import jax
import jax.numpy as jnp
from jax import lax
from jax.experimental import pallas as pl
from jax.experimental.pallas import tpu as pltpu
from jax.sharding import PartitionSpec as P

MESH = pl.DeviceIdType.MESH
SIDE = 4
ROWS = 64
COLS = 128
HALF = ROWS // 2
BLOCK = SIDE * SIDE * ROWS
FIRST = (0, 1, 3, 5, 9)
COUNT = (1, 2, 2, 4, 4)
BLOCKS = 13
F32, BF16 = jnp.float32, jnp.bfloat16


def split(values):
    high = values.astype(BF16)
    low = (values - high.astype(F32)).astype(BF16)
    return high, low


class Copies:
    def __init__(self, send, recv):
        self.send, self.recv, self.used, self.sent = send, recv, 0, []

    def slot(self):
        self.used += 1
        return self.used - 1

    def start(self, slot, src, dst, device):
        copy = pltpu.make_async_remote_copy(
            src_ref=src, dst_ref=dst, send_sem=self.send.at[slot], recv_sem=self.recv.at[slot],
            device_id=device, device_id_type=MESH,
        )
        copy.start()
        self.sent.append(copy)

    def arrived(self, slot, dst, device):
        pltpu.make_async_remote_copy(
            src_ref=dst, dst_ref=dst, send_sem=self.send.at[slot], recv_sem=self.recv.at[slot],
            device_id=device, device_id_type=MESH,
        ).wait_recv()

    def finish(self):
        for copy in self.sent:
            copy.wait_send()


def kernel(
    sides, leaf, mid, top, cmid, ctop, pmid, ptop, out,
    raw_leaf, raw_cmid, raw_mid, raw_ctop, raw_top, halves, sibling_half, rows_cat, cols_cat,
    gathered, partial, recv_first, recv_second, reduced, recv_cube, mine, cross, local_sem, send, recv,
):
    cube = lax.axis_index("cube")
    front = lax.axis_index("front")
    core = lax.rem(front, 2)
    ypos = lax.rem(front // 2, SIDE)
    xpos = front // (2 * SIDE)

    def at(x, y, z, c):
        return (z, (x * SIDE + y) * 2 + c)

    def along_x(by):
        return at(lax.rem(xpos + by, SIDE), ypos, cube, core)

    def along_y(by):
        return at(xpos, lax.rem(ypos + by, SIDE), cube, core)

    def along_z(by, members):
        member = lax.rem(cube, members)
        return at(xpos, ypos, cube - member + lax.rem(member + by, members), core)

    sibling = at(xpos, ypos, cube, 1 - core)
    copies = Copies(send, recv)

    raws = (raw_leaf, raw_cmid, raw_mid, raw_ctop, raw_top)
    loads = []
    for k, (src, dst) in enumerate(zip((leaf, cmid, mid, ctop, top), raws)):
        load = pltpu.make_async_copy(src.at[0], dst, local_sem.at[k])
        load.start()
        loads.append(load)

    barrier = pltpu.get_barrier_semaphore()
    peers = [sibling]
    for by in range(1, SIDE):
        peers += [along_x(by), along_y(by), along_z(by, 4)]
    for peer in peers:
        pl.semaphore_signal(barrier, inc=1, device_id=peer, device_id_type=MESH)
    pl.semaphore_wait(barrier, len(peers))

    lane = lax.broadcasted_iota(jnp.int32, (ROWS, 128), 1)
    first_half = lane < ROWS

    half_slots = {}

    def halve(k, pattern):
        loads[k].wait()

        def one(m, carry):
            for i in range(BLOCK // 128):
                at_column = pl.multiple_of(m * (2 * BLOCK) + i * 256, 256)
                left = raws[k][:, pl.ds(at_column, 128)]
                right = raws[k][:, pl.ds(at_column + 128, 128)]
                low = jnp.where(first_half, left, pltpu.roll(right, ROWS, 1))
                high = jnp.where(first_half, pltpu.roll(left, ROWS, 1), right)
                if pattern is not None:
                    tile = m * (2 * BLOCK // ROWS) + 4 * i
                    keep = [pattern[0, 0, tile + j].astype(F32) for j in range(4)]
                    low = low * jnp.where(first_half, keep[0], keep[2])
                    high = high * jnp.where(first_half, keep[1], keep[3])
                halves[0, FIRST[k] + m, :, i * 128 : (i + 1) * 128] = low
                halves[1, FIRST[k] + m, :, i * 128 : (i + 1) * 128] = high
            return carry

        lax.fori_loop(0, COUNT[k], one, 0)
        where = pl.ds(FIRST[k], COUNT[k])
        half_slots[k] = copies.slot()
        copies.start(half_slots[k], halves.at[1 - core, where], sibling_half.at[where], sibling)

    def fill_rows(k):
        where = pl.ds(FIRST[k], COUNT[k])
        copies.arrived(half_slots[k], sibling_half.at[where], sibling)

        def one(m, carry):
            blk = FIRST[k] + m
            for first, source in ((0, halves[core, blk]), (ROWS, sibling_half[blk])):
                high, low = split(source)
                rows_cat[blk, first : first + ROWS] = high
                rows_cat[blk, 2 * ROWS + first : 3 * ROWS + first] = low
            return carry

        lax.fori_loop(0, COUNT[k], one, 0)

    def fill_cols(k):
        def one(m, carry):
            blk = FIRST[k] + m
            for i in range(BLOCK // 128):
                part = slice(i * 128, (i + 1) * 128)
                both = jnp.concatenate([halves[core, blk, :, part], sibling_half[blk, :, part]], 0)
                high, low = split(both.T)
                cols_cat[blk, part, :128] = high
                cols_cat[blk, part, 128:] = low
            return carry

        lax.fori_loop(0, COUNT[k], one, 0)

    def gather_product(k, shard, early, late):
        first, members = FIRST[k], COUNT[k]
        member = lax.rem(cube, members)
        gathered[first, xpos, ypos] = shard
        groups = [(first, 1)] + ([(first + 1, members - 1)] if members > 1 else [])
        z_slots = [copies.slot() for _ in range(1, members)]
        for by in range(1, members):
            copies.start(
                z_slots[by - 1], gathered.at[first, xpos, ypos],
                gathered.at[first + members - by, xpos, ypos], along_z(by, members),
            )
        ring_slots = [[(copies.slot(), copies.slot()) for _ in range(1, SIDE)] for _ in groups]
        next_slots = [
            [[(copies.slot(), copies.slot()) for _ in range(1, SIDE)] for _ in range(1, SIDE)] for _ in groups
        ]

        def to_rings(g):
            where = pl.ds(*groups[g])
            block = gathered.at[where, xpos, ypos]
            for by in range(1, SIDE):
                copies.start(ring_slots[g][by - 1][0], block, block, along_x(by))
                copies.start(ring_slots[g][by - 1][1], block, block, along_y(by))

        def onward(g):
            where = pl.ds(*groups[g])
            for by in range(1, SIDE):
                x_from, y_from = lax.rem(xpos + SIDE - by, SIDE), lax.rem(ypos + SIDE - by, SIDE)
                copies.arrived(ring_slots[g][by - 1][0], gathered.at[where, x_from, ypos], along_x(by))
                block = gathered.at[where, x_from, ypos, 0:HALF]
                for on in range(1, SIDE):
                    copies.start(next_slots[g][by - 1][on - 1][0], block, block, along_y(on))
                copies.arrived(ring_slots[g][by - 1][1], gathered.at[where, xpos, y_from], along_y(by))
                block = gathered.at[where, xpos, y_from, HALF:ROWS]
                for on in range(1, SIDE):
                    copies.start(next_slots[g][by - 1][on - 1][1], block, block, along_x(on))

        def all_in(g):
            where = pl.ds(*groups[g])
            for by in range(1, SIDE):
                for on in range(1, SIDE):
                    x_from, y_from = lax.rem(xpos + SIDE - by, SIDE), lax.rem(ypos + SIDE - on, SIDE)
                    copies.arrived(
                        next_slots[g][by - 1][on - 1][0], gathered.at[where, x_from, y_from, 0:HALF], along_y(on)
                    )
                    x_from, y_from = lax.rem(xpos + SIDE - on, SIDE), lax.rem(ypos + SIDE - by, SIDE)
                    copies.arrived(
                        next_slots[g][by - 1][on - 1][1], gathered.at[where, x_from, y_from, HALF:ROWS], along_x(on)
                    )

        def multiply(d):
            vectors = gathered[first + d].reshape(BLOCK, COLS)
            both = jnp.concatenate(split(vectors), 1)
            blk = first + lax.rem(member + d, members)
            return jnp.dot(rows_cat[blk], both, preferred_element_type=F32)

        to_rings(0)
        early()
        if members > 1:
            for by in range(1, members):
                copies.arrived(
                    z_slots[by - 1], gathered.at[first + members - by, xpos, ypos], along_z(by, members)
                )
            to_rings(1)
        for g in range(len(groups)):
            onward(g)
        late()
        all_in(0)
        total = multiply(0)
        if members > 1:
            all_in(1)
            for d in range(1, members):
                total = total + multiply(d)
        total = total[:, :COLS] + total[:, COLS:]
        total = total[: 2 * ROWS] + total[2 * ROWS :]
        cross[k, 0] = total[ROWS:]
        slot = copies.slot()
        copies.start(slot, cross.at[k, 0], cross.at[k, 1], sibling)
        copies.arrived(slot, cross.at[k, 1], sibling)
        return total[:ROWS] + cross[k, 1]

    def spread_product(k, shard):
        first, members = FIRST[k], COUNT[k]
        member = lax.rem(cube, members)
        mine[k, 0] = shard
        slot = copies.slot()
        copies.start(slot, mine.at[k, 0], mine.at[k, 1], sibling)
        copies.arrived(slot, mine.at[k, 1], sibling)
        high, low = split(mine[k].reshape(2 * ROWS, COLS))
        vectors = jnp.concatenate([high, low], 1)
        vectors = jnp.concatenate([vectors, vectors], 0)
        groups = ([(first + 1, members - 1)] if members > 1 else []) + [(first, 1)]
        first_slots = [[(copies.slot(), copies.slot()) for _ in range(1, SIDE)] for _ in groups]
        second_slots = [[(copies.slot(), copies.slot()) for _ in range(1, SIDE)] for _ in groups]
        z_slots = [copies.slot() for _ in range(1, members)]

        for g, (begin, size) in enumerate(groups):
            for d in range(begin - first, begin - first + size):
                blk = first + lax.rem(member + d, members)
                product = jnp.dot(cols_cat[blk], vectors, preferred_element_type=F32)
                product = product[:, :COLS] + product[:, COLS:]
                partial[first + d] = product.reshape(SIDE, SIDE, ROWS, COLS)
            where = pl.ds(begin, size)
            for by in range(1, SIDE):
                copies.start(
                    first_slots[g][by - 1][0], partial.at[where, :, lax.rem(ypos + by, SIDE), 0:HALF],
                    recv_first.at[0, by - 1, where], along_y(by),
                )
                copies.start(
                    first_slots[g][by - 1][1], partial.at[where, lax.rem(xpos + by, SIDE), :, HALF:ROWS],
                    recv_first.at[1, by - 1, where], along_x(by),
                )

        for g, (begin, size) in enumerate(groups):
            where = pl.ds(begin, size)
            for by in range(1, SIDE):
                copies.arrived(first_slots[g][by - 1][0], recv_first.at[0, by - 1, where], along_y(by))
                copies.arrived(first_slots[g][by - 1][1], recv_first.at[1, by - 1, where], along_x(by))
            for b in range(begin, begin + size):
                upper = partial[b, :, ypos, 0:HALF]
                lower = partial[b, xpos, :, HALF:ROWS]
                for by in range(SIDE - 1):
                    upper = upper + recv_first[0, by, b]
                    lower = lower + recv_first[1, by, b]
                reduced[0, b] = upper
                reduced[1, b] = lower
            for by in range(1, SIDE):
                copies.start(
                    second_slots[g][by - 1][0], reduced.at[0, where, lax.rem(xpos + by, SIDE)],
                    recv_second.at[by - 1, where, 0:HALF], along_x(by),
                )
                copies.start(
                    second_slots[g][by - 1][1], reduced.at[1, where, lax.rem(ypos + by, SIDE)],
                    recv_second.at[by - 1, where, HALF:ROWS], along_y(by),
                )

        for g, (begin, size) in enumerate(groups):
            where = pl.ds(begin, size)
            for by in range(1, SIDE):
                copies.arrived(second_slots[g][by - 1][0], recv_second.at[by - 1, where, 0:HALF], along_x(by))
                copies.arrived(second_slots[g][by - 1][1], recv_second.at[by - 1, where, HALF:ROWS], along_y(by))
            for b in range(begin, begin + size):
                total = jnp.concatenate([reduced[0, b, xpos], reduced[1, b, ypos]], 0)
                for by in range(SIDE - 1):
                    total = total + recv_second[by, b]
                if b == first:
                    own = total
                else:
                    by = b - first
                    recv_cube[0, b] = total
                    copies.start(z_slots[by - 1], recv_cube.at[0, b], recv_cube.at[1, b], along_z(by, members))
        for by in range(1, members):
            copies.arrived(z_slots[by - 1], recv_cube.at[1, first + by], along_z(by, members))
            own = own + recv_cube[1, first + by]
        return own

    def nothing():
        pass

    def all_of(*steps):
        def run():
            for step, *which in steps:
                step(*which)

        return run

    solved_leaf = gather_product(
        0, sides[0, 0],
        all_of((halve, 0, None), (halve, 1, pmid), (halve, 2, None)),
        all_of((halve, 3, ptop), (halve, 4, None), (fill_rows, 0)),
    )
    update_mid = gather_product(1, solved_leaf, all_of((fill_rows, 1)), all_of((fill_rows, 2)))
    solved_mid = gather_product(2, sides[1, 0] - update_mid, nothing, all_of((fill_rows, 3), (fill_cols, 0)))
    update_top = gather_product(3, solved_mid, nothing, all_of((fill_rows, 4), (fill_cols, 1), (fill_cols, 2)))
    solved_top = gather_product(4, sides[2, 0] - update_top, nothing, all_of((fill_cols, 4), (fill_cols, 3)))
    back_top = spread_product(4, solved_top)
    out[2, 0] = back_top
    carry_mid = spread_product(3, back_top)
    back_mid = spread_product(2, solved_mid - carry_mid)
    out[1, 0] = back_mid
    carry_leaf = spread_product(1, back_mid)
    back_leaf = spread_product(0, solved_leaf - carry_leaf)
    out[0, 0] = back_leaf
    copies.finish()


def local(right_sides, inverse_leaf, inverse_mid, inverse_top, coupling_mid, coupling_top, pattern_mid, pattern_top):
    n_copies = 420
    vmem = pl.BlockSpec(memory_space=pltpu.VMEM)
    smem = pl.BlockSpec(memory_space=pltpu.SMEM)
    hbm = pl.BlockSpec(memory_space=pl.ANY)
    return pl.pallas_call(
        kernel,
        out_shape=jax.ShapeDtypeStruct(right_sides.shape, F32),
        in_specs=[vmem, hbm, hbm, hbm, hbm, hbm, smem, smem],
        out_specs=vmem,
        scratch_shapes=[
            *[pltpu.VMEM((ROWS, 2 * BLOCK * count), F32) for count in COUNT],
            pltpu.VMEM((2, BLOCKS, ROWS, BLOCK), F32),
            pltpu.VMEM((BLOCKS, ROWS, BLOCK), F32),
            pltpu.VMEM((BLOCKS, 4 * ROWS, BLOCK), BF16),
            pltpu.VMEM((BLOCKS, BLOCK, 4 * ROWS), BF16),
            pltpu.VMEM((BLOCKS, SIDE, SIDE, ROWS, COLS), F32),
            pltpu.VMEM((BLOCKS, SIDE, SIDE, ROWS, COLS), F32),
            pltpu.VMEM((2, SIDE - 1, BLOCKS, SIDE, HALF, COLS), F32),
            pltpu.VMEM((SIDE - 1, BLOCKS, ROWS, COLS), F32),
            pltpu.VMEM((2, BLOCKS, SIDE, HALF, COLS), F32),
            pltpu.VMEM((2, BLOCKS, ROWS, COLS), F32),
            pltpu.VMEM((5, 2, ROWS, COLS), F32),
            pltpu.VMEM((5, 2, ROWS, COLS), F32),
            pltpu.SemaphoreType.DMA((5,)),
            pltpu.SemaphoreType.DMA((n_copies,)),
            pltpu.SemaphoreType.DMA((n_copies,)),
        ],
        compiler_params=pltpu.CompilerParams(
            collective_id=0, has_side_effects=True, vmem_limit_bytes=62 * 2**20
        ),
        name="solve",
    )(right_sides, inverse_leaf, inverse_mid, inverse_top, coupling_mid, coupling_top, pattern_mid, pattern_top)


def solution(mesh):
    split_rows = P("cube", "front", None)
    levels = P(None, "cube", "front", None)
    return jax.shard_map(
        local, mesh=mesh, in_specs=(levels,) + (split_rows,) * 7, out_specs=levels, check_vma=False,
    )
```

```python
import functools

import jax
import jax.numpy as jnp
from jax import lax
from jax.experimental import pallas as pl
from jax.experimental.pallas import tpu as pltpu
from jax.sharding import PartitionSpec as P

MESH = pl.DeviceIdType.MESH
SIDE = 4
ROWS = 64
COLS = 128
CHAINS = 2
PACK = ROWS // CHAINS
HALF = PACK // 2
BLOCK = SIDE * SIDE * ROWS
FIRST = (0, 1, 3, 5, 9)
COUNT = (1, 2, 2, 4, 4)
BLOCKS = 13
LAG = 1
F32, BF16 = jnp.float32, jnp.bfloat16


def split(values):
    high = values.astype(BF16)
    low = (values - high.astype(F32)).astype(BF16)
    return high, low


def left_lanes(values):
    return lax.broadcasted_iota(jnp.int32, values.shape, values.ndim - 1) < COLS // 2


def side_by_side(packed):
    flat = packed.reshape(-1, COLS)
    turned = pltpu.roll(flat, COLS // 2, 1)
    left = left_lanes(flat)
    high, low = flat.astype(BF16).astype(F32), turned - turned.astype(BF16).astype(F32)
    upper = jnp.where(left, high, low).astype(BF16)
    high, low = turned.astype(BF16).astype(F32), flat - flat.astype(BF16).astype(F32)
    lower = jnp.where(left, high, low).astype(BF16)
    both = jnp.concatenate([upper.reshape(packed.shape), lower.reshape(packed.shape)], 1)
    return both.reshape(-1, COLS)


def packed_sum(product):
    total = (product + pltpu.roll(product, COLS // 2, 1)).reshape(-1, ROWS, COLS)
    upper, lower = total[:, :PACK], total[:, PACK:]
    return jnp.where(left_lanes(upper), upper, lower)


def packed(values, chain):
    upper, lower = values[:PACK], values[PACK:]
    if chain == 0:
        return jnp.where(left_lanes(upper), upper, pltpu.roll(lower, COLS // 2, 1))
    return jnp.where(left_lanes(upper), pltpu.roll(upper, COLS // 2, 1), lower)


def unpacked(first, second):
    left = left_lanes(first)
    upper = jnp.where(left, first, pltpu.roll(second, COLS // 2, 1))
    lower = jnp.where(left, pltpu.roll(first, COLS // 2, 1), second)
    return jnp.concatenate([upper, lower], 0)


class Copies:
    def __init__(self, send, recv):
        self.send, self.recv, self.used = send, recv, 0

    def slot(self):
        self.used += 1
        assert self.used <= RECEIVE
        return self.used - 1

    def start(self, group, slot, src, dst, device):
        pltpu.make_async_remote_copy(
            src_ref=src, dst_ref=dst, send_sem=self.send.at[group], recv_sem=self.recv.at[slot],
            device_id=device, device_id_type=MESH,
        ).start()

    def arrived(self, slot, dst, device):
        pltpu.make_async_remote_copy(
            src_ref=dst, dst_ref=dst, send_sem=self.send.at[0], recv_sem=self.recv.at[slot],
            device_id=device, device_id_type=MESH,
        ).wait_recv()

    def all_sent(self, group, as_many, device):
        pltpu.make_async_remote_copy(
            src_ref=as_many, dst_ref=as_many, send_sem=self.send.at[group], recv_sem=self.recv.at[0],
            device_id=device, device_id_type=MESH,
        ).wait_send()


SENDS = CHAINS * 10 + 1
RECEIVE = 203


def kernel(
    sides, leaf, mid, top, cmid, ctop, pmid, ptop, out,
    raw_leaf, raw_cmid, raw_mid, raw_ctop, raw_top, halves, sibling_half, rows_cat, cols_cat,
    gathered, partial, recv_first, recv_second, reduced, recv_cube, mine, cross, result, local_sem, send, recv,
):
    cube = lax.axis_index("cube")
    front = lax.axis_index("front")
    core = lax.rem(front, 2)
    ypos = lax.rem(front // 2, SIDE)
    xpos = front // (2 * SIDE)

    def at(x, y, z, c):
        return (z, (x * SIDE + y) * 2 + c)

    def along_x(by):
        return at(lax.rem(xpos + by, SIDE), ypos, cube, core)

    def along_y(by):
        return at(xpos, lax.rem(ypos + by, SIDE), cube, core)

    def along_z(by, members):
        member = lax.rem(cube, members)
        return at(xpos, ypos, cube - member + lax.rem(member + by, members), core)

    sibling = at(xpos, ypos, cube, 1 - core)
    copies = Copies(send, recv)

    raws = (raw_leaf, raw_cmid, raw_mid, raw_ctop, raw_top)
    loads = []
    for k, (src, dst) in enumerate(zip((leaf, cmid, mid, ctop, top), raws)):
        load = pltpu.make_async_copy(src.at[0], dst, local_sem.at[k])
        load.start()
        loads.append(load)

    barrier = pltpu.get_barrier_semaphore()
    peers = [sibling]
    for by in range(1, SIDE):
        peers += [along_x(by), along_y(by), along_z(by, 4)]
    for peer in peers:
        pl.semaphore_signal(barrier, inc=1, device_id=peer, device_id_type=MESH)
    pl.semaphore_wait(barrier, len(peers))

    lane = lax.broadcasted_iota(jnp.int32, (ROWS, 128), 1)
    first_half = lane < ROWS

    half_slots = {}

    def halve(k, pattern):
        loads[k].wait()

        def one(m, carry):
            for i in range(BLOCK // 128):
                at_column = pl.multiple_of(m * (2 * BLOCK) + i * 256, 256)
                left = raws[k][:, pl.ds(at_column, 128)]
                right = raws[k][:, pl.ds(at_column + 128, 128)]
                low = jnp.where(first_half, left, pltpu.roll(right, ROWS, 1))
                high = jnp.where(first_half, pltpu.roll(left, ROWS, 1), right)
                if pattern is not None:
                    tile = m * (2 * BLOCK // ROWS) + 4 * i
                    keep = [pattern[0, 0, tile + j].astype(F32) for j in range(4)]
                    low = low * jnp.where(first_half, keep[0], keep[2])
                    high = high * jnp.where(first_half, keep[1], keep[3])
                halves[0, FIRST[k] + m, :, i * 128 : (i + 1) * 128] = low
                halves[1, FIRST[k] + m, :, i * 128 : (i + 1) * 128] = high
            return carry

        lax.fori_loop(0, COUNT[k], one, 0)
        where = pl.ds(FIRST[k], COUNT[k])
        half_slots[k] = copies.slot()
        copies.start(SENDS - 1, half_slots[k], halves.at[1 - core, where], sibling_half.at[where], sibling)

    def fill_rows(k):
        copies.arrived(half_slots[k], sibling_half.at[pl.ds(FIRST[k], COUNT[k])], sibling)

        def one(m, carry):
            blk = FIRST[k] + m
            for first, source in ((0, halves[core, blk]), (ROWS, sibling_half[blk])):
                high, low = split(source)
                rows_cat[blk, first : first + ROWS] = high
                rows_cat[blk, 2 * ROWS + first : 3 * ROWS + first] = low
            return carry

        lax.fori_loop(0, COUNT[k], one, 0)

    def fill_cols(k):
        def one(m, carry):
            blk = FIRST[k] + m
            for i in range(BLOCK // 128):
                part = slice(i * 128, (i + 1) * 128)
                both = jnp.concatenate([halves[core, blk, :, part], sibling_half[blk, :, part]], 0)
                high, low = split(both.T)
                cols_cat[blk, part, :128] = high
                cols_cat[blk, part, 128:] = low
            return carry

        lax.fori_loop(0, COUNT[k], one, 0)

    def gather_product(c, k, shard, early=None, late=None):
        first, members = FIRST[k], COUNT[k]
        member = lax.rem(cube, members)
        group = c * 10 + k
        gathered[c, first, xpos, ypos] = shard
        groups = [(first, 1)] + ([(first + 1, members - 1)] if members > 1 else [])
        z_slot = copies.slot() if members > 1 else None
        for by in range(1, members):
            copies.start(
                group, z_slot, gathered.at[c, first, xpos, ypos],
                gathered.at[c, first + members - by, xpos, ypos], along_z(by, members),
            )
        ring_slots = [[(copies.slot(), copies.slot()) for _ in range(1, SIDE)] for _ in groups]
        next_slots = [copies.slot() for _ in groups]

        def to_rings(g):
            where = pl.ds(*groups[g])
            block = gathered.at[c, where, xpos, ypos]
            for by in range(1, SIDE):
                copies.start(group, ring_slots[g][by - 1][0], block, block, along_x(by))
                copies.start(group, ring_slots[g][by - 1][1], block, block, along_y(by))

        def onward(g):
            where = pl.ds(*groups[g])
            for by in (1, 3, 2):
                x_from, y_from = lax.rem(xpos + SIDE - by, SIDE), lax.rem(ypos + SIDE - by, SIDE)
                copies.arrived(ring_slots[g][by - 1][0], gathered.at[c, where, x_from, ypos], along_x(by))
                block = gathered.at[c, where, x_from, ypos, 0:HALF]
                for on in range(1, SIDE):
                    copies.start(group, next_slots[g], block, block, along_y(on))
                copies.arrived(ring_slots[g][by - 1][1], gathered.at[c, where, xpos, y_from], along_y(by))
                block = gathered.at[c, where, xpos, y_from, HALF:PACK]
                for on in range(1, SIDE):
                    copies.start(group, next_slots[g], block, block, along_x(on))

        def multiply(d):
            vectors = side_by_side(gathered[c, first + d].reshape(SIDE * SIDE, PACK, COLS))
            blk = first + lax.rem(member + d, members)
            return jnp.dot(rows_cat[blk], vectors, preferred_element_type=F32)

        to_rings(0)
        if early:
            early()
        yield
        if members > 1:
            copies.arrived(z_slot, gathered.at[c, pl.ds(first + 1, members - 1), xpos, ypos], sibling)
            to_rings(1)
            yield
        for g in range(len(groups)):
            onward(g)
        if late:
            late()
        yield
        total = None
        for g, (begin, size) in enumerate(groups):
            copies.arrived(next_slots[g], gathered.at[c, pl.ds(begin, size), 0 : SIDE - 1, 0 : SIDE - 1], sibling)
            for d in range(begin - first, begin - first + size):
                term = multiply(d)
                total = term if total is None else total + term
        total = packed_sum(total[: 2 * ROWS] + total[2 * ROWS :])
        cross[c, k, 0] = total[1]
        slot = copies.slot()
        copies.start(group, slot, cross.at[c, k, 0], cross.at[c, k, 1], sibling)
        copies.arrived(slot, cross.at[c, k, 1], sibling)
        return total[0] + cross[c, k, 1]

    def spread_product(c, k, shard):
        first, members = FIRST[k], COUNT[k]
        member = lax.rem(cube, members)
        group = c * 10 + 5 + k
        mine[c, k, 0] = shard
        slot = copies.slot()
        copies.start(group, slot, mine.at[c, k, 0], mine.at[c, k, 1], sibling)
        groups = ([(first + 1, members - 1)] if members > 1 else []) + [(first, 1)]
        first_slots = [copies.slot() for _ in groups]
        second_slots = [copies.slot() for _ in groups]
        z_slot = copies.slot() if members > 1 else None
        copies.arrived(slot, mine.at[c, k, 1], sibling)
        vectors = side_by_side(mine[c, k])
        vectors = jnp.concatenate([vectors, vectors], 0)
        for g, (begin, size) in enumerate(groups):
            for d in range(begin - first, begin - first + size):
                blk = first + lax.rem(member + d, members)
                product = packed_sum(jnp.dot(cols_cat[blk], vectors, preferred_element_type=F32))
                partial[c, first + d] = product.reshape(SIDE, SIDE, PACK, COLS)
            where = pl.ds(begin, size)
            for by in range(1, SIDE):
                copies.start(
                    group, first_slots[g], partial.at[c, where, :, lax.rem(ypos + by, SIDE), 0:HALF],
                    recv_first.at[c, 0, by - 1, where], along_y(by),
                )
                copies.start(
                    group, first_slots[g], partial.at[c, where, lax.rem(xpos + by, SIDE), :, HALF:PACK],
                    recv_first.at[c, 1, by - 1, where], along_x(by),
                )
        yield
        for g, (begin, size) in enumerate(groups):
            where = pl.ds(begin, size)
            copies.arrived(first_slots[g], recv_first.at[c, :, :, where], sibling)
            for b in range(begin, begin + size):
                upper = partial[c, b, :, ypos, 0:HALF]
                lower = partial[c, b, xpos, :, HALF:PACK]
                for by in range(SIDE - 1):
                    upper = upper + recv_first[c, 0, by, b]
                    lower = lower + recv_first[c, 1, by, b]
                reduced[c, 0, b] = upper
                reduced[c, 1, b] = lower
            for by in range(1, SIDE):
                copies.start(
                    group, second_slots[g], reduced.at[c, 0, where, lax.rem(xpos + by, SIDE)],
                    recv_second.at[c, by - 1, where, 0:HALF], along_x(by),
                )
                copies.start(
                    group, second_slots[g], reduced.at[c, 1, where, lax.rem(ypos + by, SIDE)],
                    recv_second.at[c, by - 1, where, HALF:PACK], along_y(by),
                )
        yield
        for g, (begin, size) in enumerate(groups):
            where = pl.ds(begin, size)
            copies.arrived(second_slots[g], recv_second.at[c, :, where], sibling)
            for b in range(begin, begin + size):
                total = jnp.concatenate([reduced[c, 0, b, xpos], reduced[c, 1, b, ypos]], 0)
                for by in range(SIDE - 1):
                    total = total + recv_second[c, by, b]
                if b == first:
                    own = total
                else:
                    recv_cube[c, 0, b] = total
                    copies.start(group, z_slot, recv_cube.at[c, 0, b], recv_cube.at[c, 1, b], along_z(b - first, members))
        if members > 1:
            yield
            copies.arrived(z_slot, recv_cube.at[c, 1, pl.ds(first + 1, members - 1)], sibling)
            for by in range(1, members):
                own = own + recv_cube[c, 1, first + by]
        return own

    def all_of(*steps):
        def run():
            for step, *which in steps:
                step(*which)

        return run

    def chain(c):
        def when_first(*steps):
            return all_of(*steps) if c == 0 else None

        solved_leaf = yield from gather_product(
            c, 0, packed(sides[0, 0], c), when_first((halve, 0, None), (halve, 1, pmid)),
            when_first((halve, 2, None), (fill_rows, 0)),
        )
        update_mid = yield from gather_product(
            c, 1, solved_leaf, when_first((fill_rows, 1),), when_first((halve, 3, ptop), (fill_rows, 2))
        )
        solved_mid = yield from gather_product(
            c, 2, packed(sides[1, 0], c) - update_mid, None, when_first((halve, 4, None), (fill_rows, 3))
        )
        update_top = yield from gather_product(
            c, 3, solved_mid, None, when_first((fill_rows, 4), (fill_cols, 0), (fill_cols, 1), (fill_cols, 2))
        )
        solved_top = yield from gather_product(
            c, 4, packed(sides[2, 0], c) - update_top, None, when_first((fill_cols, 4), (fill_cols, 3))
        )
        result[c, 2] = yield from spread_product(c, 4, solved_top)
        carry_mid = yield from spread_product(c, 3, result[c, 2])
        result[c, 1] = yield from spread_product(c, 2, solved_mid - carry_mid)
        carry_leaf = yield from spread_product(c, 1, result[c, 1])
        result[c, 0] = yield from spread_product(c, 0, solved_leaf - carry_leaf)

    chains = [chain(c) for c in range(CHAINS)]
    for _ in range(LAG):
        next(chains[0])
    done = object()
    while chains:
        chains = [one for one in reversed(chains) if next(one, done) is not done][::-1]
    for level in range(3):
        out[level, 0] = unpacked(result[0, level], result[1, level])
    copies.all_sent(SENDS - 1, sibling_half, sibling)
    for c in range(CHAINS):
        for k in range(5):
            where = pl.ds(FIRST[k], COUNT[k])
            copies.all_sent(c * 10 + k, gathered.at[c, where], sibling)
            copies.all_sent(c * 10 + 5 + k, partial.at[c, where], sibling)


def local(right_sides, inverse_leaf, inverse_mid, inverse_top, coupling_mid, coupling_top, pattern_mid, pattern_top):
    vmem = pl.BlockSpec(memory_space=pltpu.VMEM)
    smem = pl.BlockSpec(memory_space=pltpu.SMEM)
    hbm = pl.BlockSpec(memory_space=pl.ANY)
    return pl.pallas_call(
        kernel,
        out_shape=jax.ShapeDtypeStruct(right_sides.shape, F32),
        in_specs=[vmem, hbm, hbm, hbm, hbm, hbm, smem, smem],
        out_specs=vmem,
        scratch_shapes=[
            *[pltpu.VMEM((ROWS, 2 * BLOCK * count), F32) for count in COUNT],
            pltpu.VMEM((2, BLOCKS, ROWS, BLOCK), F32),
            pltpu.VMEM((BLOCKS, ROWS, BLOCK), F32),
            pltpu.VMEM((BLOCKS, 4 * ROWS, BLOCK), BF16),
            pltpu.VMEM((BLOCKS, BLOCK, 4 * ROWS), BF16),
            pltpu.VMEM((CHAINS, BLOCKS, SIDE, SIDE, PACK, COLS), F32),
            pltpu.VMEM((CHAINS, BLOCKS, SIDE, SIDE, PACK, COLS), F32),
            pltpu.VMEM((CHAINS, 2, SIDE - 1, BLOCKS, SIDE, HALF, COLS), F32),
            pltpu.VMEM((CHAINS, SIDE - 1, BLOCKS, PACK, COLS), F32),
            pltpu.VMEM((CHAINS, 2, BLOCKS, SIDE, HALF, COLS), F32),
            pltpu.VMEM((CHAINS, 2, BLOCKS, PACK, COLS), F32),
            pltpu.VMEM((CHAINS, 5, 2, PACK, COLS), F32),
            pltpu.VMEM((CHAINS, 5, 2, PACK, COLS), F32),
            pltpu.VMEM((CHAINS, 3, PACK, COLS), F32),
            pltpu.SemaphoreType.DMA((5,)),
            pltpu.SemaphoreType.DMA((SENDS,)),
            pltpu.SemaphoreType.DMA((RECEIVE,)),
        ],
        compiler_params=pltpu.CompilerParams(
            collective_id=0, has_side_effects=True, vmem_limit_bytes=62 * 2**20
        ),
        name="solve",
    )(right_sides, inverse_leaf, inverse_mid, inverse_top, coupling_mid, coupling_top, pattern_mid, pattern_top)


def solution(mesh):
    split_rows = P("cube", "front", None)
    levels = P(None, "cube", "front", None)
    return jax.shard_map(
        local, mesh=mesh, in_specs=(levels,) + (split_rows,) * 7, out_specs=levels, check_vma=False,
    )
```

```python
import functools

import jax
import jax.numpy as jnp
from jax import lax
from jax.experimental import pallas as pl
from jax.experimental.pallas import tpu as pltpu
from jax.sharding import PartitionSpec as P

MESH = pl.DeviceIdType.MESH
SIDE = 4
ROWS = 64
COLS = 128
CHAINS = 2
PACK = ROWS // CHAINS
HALF = PACK // 2
BLOCK = SIDE * SIDE * ROWS
FIRST = (0, 1, 3, 5, 9)
COUNT = (1, 2, 2, 4, 4)
BLOCKS = 13
TURNS = ((1, 3), (2,))
LAG = 1
F32, BF16 = jnp.float32, jnp.bfloat16


def split(values):
    high = values.astype(BF16)
    low = (values - high.astype(F32)).astype(BF16)
    return high, low


def left_lanes(values):
    return lax.broadcasted_iota(jnp.int32, values.shape, values.ndim - 1) < COLS // 2


def side_by_side(packed):
    flat = packed.reshape(-1, COLS)
    turned = pltpu.roll(flat, COLS // 2, 1)
    left = left_lanes(flat)
    high, low = flat.astype(BF16).astype(F32), turned - turned.astype(BF16).astype(F32)
    upper = jnp.where(left, high, low).astype(BF16)
    high, low = turned.astype(BF16).astype(F32), flat - flat.astype(BF16).astype(F32)
    lower = jnp.where(left, high, low).astype(BF16)
    both = jnp.concatenate([upper.reshape(packed.shape), lower.reshape(packed.shape)], 1)
    return both.reshape(-1, COLS)


def packed_sum(product):
    total = (product + pltpu.roll(product, COLS // 2, 1)).reshape(-1, ROWS, COLS)
    upper, lower = total[:, :PACK], total[:, PACK:]
    return jnp.where(left_lanes(upper), upper, lower)


def packed(values, chain):
    upper, lower = values[:PACK], values[PACK:]
    if chain == 0:
        return jnp.where(left_lanes(upper), upper, pltpu.roll(lower, COLS // 2, 1))
    return jnp.where(left_lanes(upper), pltpu.roll(upper, COLS // 2, 1), lower)


def unpacked(first, second):
    left = left_lanes(first)
    upper = jnp.where(left, first, pltpu.roll(second, COLS // 2, 1))
    lower = jnp.where(left, pltpu.roll(first, COLS // 2, 1), second)
    return jnp.concatenate([upper, lower], 0)


class Copies:
    def __init__(self, send, recv):
        self.send, self.recv, self.used = send, recv, 0

    def slot(self):
        self.used += 1
        assert self.used <= RECEIVE
        return self.used - 1

    def start(self, group, slot, src, dst, device):
        pltpu.make_async_remote_copy(
            src_ref=src, dst_ref=dst, send_sem=self.send.at[group], recv_sem=self.recv.at[slot],
            device_id=device, device_id_type=MESH,
        ).start()

    def arrived(self, slot, dst, device):
        pltpu.make_async_remote_copy(
            src_ref=dst, dst_ref=dst, send_sem=self.send.at[0], recv_sem=self.recv.at[slot],
            device_id=device, device_id_type=MESH,
        ).wait_recv()

    def all_sent(self, group, as_many, device):
        pltpu.make_async_remote_copy(
            src_ref=as_many, dst_ref=as_many, send_sem=self.send.at[group], recv_sem=self.recv.at[0],
            device_id=device, device_id_type=MESH,
        ).wait_send()


SENDS = CHAINS * 10 + 1
RECEIVE = 131


def kernel(
    sides, leaf, mid, top, cmid, ctop, pmid, ptop, out,
    raw_leaf, raw_cmid, raw_mid, raw_ctop, raw_top, halves, sibling_half, rows_cat, cols_cat,
    gathered, partial, recv_first, recv_second, reduced, recv_cube, mine, cross, result, local_sem, send, recv,
):
    cube = lax.axis_index("cube")
    front = lax.axis_index("front")
    core = lax.rem(front, 2)
    ypos = lax.rem(front // 2, SIDE)
    xpos = front // (2 * SIDE)

    def at(x, y, z, c):
        return (z, (x * SIDE + y) * 2 + c)

    def along_x(by):
        return at(lax.rem(xpos + by, SIDE), ypos, cube, core)

    def along_y(by):
        return at(xpos, lax.rem(ypos + by, SIDE), cube, core)

    def along_z(by, members):
        member = lax.rem(cube, members)
        return at(xpos, ypos, cube - member + lax.rem(member + by, members), core)

    sibling = at(xpos, ypos, cube, 1 - core)
    copies = Copies(send, recv)

    raws = (raw_leaf, raw_cmid, raw_mid, raw_ctop, raw_top)
    loads = []
    for k, (src, dst) in enumerate(zip((leaf, cmid, mid, ctop, top), raws)):
        load = pltpu.make_async_copy(src.at[0], dst, local_sem.at[k])
        load.start()
        loads.append(load)

    barrier = pltpu.get_barrier_semaphore()
    peers = [sibling]
    for by in range(1, SIDE):
        peers += [along_x(by), along_y(by), along_z(by, 4)]
    for peer in peers:
        pl.semaphore_signal(barrier, inc=1, device_id=peer, device_id_type=MESH)
    pl.semaphore_wait(barrier, len(peers))

    lane = lax.broadcasted_iota(jnp.int32, (ROWS, 128), 1)
    first_half = lane < ROWS

    half_slots = {}

    def halve(k, pattern):
        loads[k].wait()

        def one(m, carry):
            for i in range(BLOCK // 128):
                at_column = pl.multiple_of(m * (2 * BLOCK) + i * 256, 256)
                left = raws[k][:, pl.ds(at_column, 128)]
                right = raws[k][:, pl.ds(at_column + 128, 128)]
                low = jnp.where(first_half, left, pltpu.roll(right, ROWS, 1))
                high = jnp.where(first_half, pltpu.roll(left, ROWS, 1), right)
                if pattern is not None:
                    tile = m * (2 * BLOCK // ROWS) + 4 * i
                    keep = [pattern[0, 0, tile + j].astype(F32) for j in range(4)]
                    low = low * jnp.where(first_half, keep[0], keep[2])
                    high = high * jnp.where(first_half, keep[1], keep[3])
                halves[0, FIRST[k] + m, :, i * 128 : (i + 1) * 128] = low
                halves[1, FIRST[k] + m, :, i * 128 : (i + 1) * 128] = high
            return carry

        lax.fori_loop(0, COUNT[k], one, 0)
        where = pl.ds(FIRST[k], COUNT[k])
        half_slots[k] = copies.slot()
        copies.start(SENDS - 1, half_slots[k], halves.at[1 - core, where], sibling_half.at[where], sibling)

    def fill_rows(k):
        copies.arrived(half_slots[k], sibling_half.at[pl.ds(FIRST[k], COUNT[k])], sibling)

        def one(m, carry):
            blk = FIRST[k] + m
            for first, source in ((0, halves[core, blk]), (ROWS, sibling_half[blk])):
                high, low = split(source)
                rows_cat[blk, first : first + ROWS] = high
                rows_cat[blk, 2 * ROWS + first : 3 * ROWS + first] = low
            return carry

        lax.fori_loop(0, COUNT[k], one, 0)

    def fill_cols(k):
        def one(m, carry):
            blk = FIRST[k] + m
            for i in range(BLOCK // 128):
                part = slice(i * 128, (i + 1) * 128)
                both = jnp.concatenate([halves[core, blk, :, part], sibling_half[blk, :, part]], 0)
                high, low = split(both.T)
                cols_cat[blk, part, :128] = high
                cols_cat[blk, part, 128:] = low
            return carry

        lax.fori_loop(0, COUNT[k], one, 0)

    def gather_product(c, k, shard, early=None, late=None):
        first, members = FIRST[k], COUNT[k]
        member = lax.rem(cube, members)
        group = c * 10 + k
        gathered[c, first, xpos, ypos] = shard
        groups = [(first, 1)] + ([(first + 1, members - 1)] if members > 1 else [])
        z_slot = copies.slot() if members > 1 else None
        for by in range(1, members):
            copies.start(
                group, z_slot, gathered.at[c, first, xpos, ypos],
                gathered.at[c, first + members - by, xpos, ypos], along_z(by, members),
            )
        ring_slots = [[copies.slot() for _ in TURNS] for _ in groups]
        next_slots = [copies.slot() for _ in groups]

        def to_rings(g):
            where = pl.ds(*groups[g])
            block = gathered.at[c, where, xpos, ypos]
            for slot, turn in zip(ring_slots[g], TURNS):
                for by in turn:
                    copies.start(group, slot, block, block, along_x(by))
                    copies.start(group, slot, block, block, along_y(by))

        def onward(g):
            where = pl.ds(*groups[g])
            for slot, turn in zip(ring_slots[g], TURNS):
                copies.arrived(slot, gathered.at[c, where, 0 : 2 * len(turn), ypos], sibling)
                for by in turn:
                    x_from, y_from = lax.rem(xpos + SIDE - by, SIDE), lax.rem(ypos + SIDE - by, SIDE)
                    block_x = gathered.at[c, where, x_from, ypos, 0:HALF]
                    block_y = gathered.at[c, where, xpos, y_from, HALF:PACK]
                    for on in (1, 3, 2):
                        copies.start(group, next_slots[g], block_x, block_x, along_y(on))
                        copies.start(group, next_slots[g], block_y, block_y, along_x(on))

        def multiply(d):
            vectors = side_by_side(gathered[c, first + d].reshape(SIDE * SIDE, PACK, COLS))
            blk = first + lax.rem(member + d, members)
            return jnp.dot(rows_cat[blk], vectors, preferred_element_type=F32)

        to_rings(0)
        if early:
            early()
        yield
        if members > 1:
            copies.arrived(z_slot, gathered.at[c, pl.ds(first + 1, members - 1), xpos, ypos], sibling)
            to_rings(1)
            onward(0)
            yield
        onward(len(groups) - 1)
        if late:
            late()
        yield
        total = None
        for g, (begin, size) in enumerate(groups):
            copies.arrived(next_slots[g], gathered.at[c, pl.ds(begin, size), 0 : SIDE - 1, 0 : SIDE - 1], sibling)
            for d in range(begin - first, begin - first + size):
                term = multiply(d)
                total = term if total is None else total + term
        total = packed_sum(total[: 2 * ROWS] + total[2 * ROWS :])
        cross[c, k, 0] = total[1]
        slot = copies.slot()
        copies.start(group, slot, cross.at[c, k, 0], cross.at[c, k, 1], sibling)
        copies.arrived(slot, cross.at[c, k, 1], sibling)
        return total[0] + cross[c, k, 1]

    def spread_product(c, k, shard):
        first, members = FIRST[k], COUNT[k]
        member = lax.rem(cube, members)
        group = c * 10 + 5 + k
        mine[c, k, 0] = shard
        slot = copies.slot()
        copies.start(group, slot, mine.at[c, k, 0], mine.at[c, k, 1], sibling)
        groups = ([(first + 1, members - 1)] if members > 1 else []) + [(first, 1)]
        first_slots = [copies.slot() for _ in groups]
        second_slots = [copies.slot() for _ in groups]
        z_slot = copies.slot() if members > 1 else None
        copies.arrived(slot, mine.at[c, k, 1], sibling)
        vectors = side_by_side(mine[c, k])
        vectors = jnp.concatenate([vectors, vectors], 0)
        for g, (begin, size) in enumerate(groups):
            for d in range(begin - first, begin - first + size):
                blk = first + lax.rem(member + d, members)
                product = packed_sum(jnp.dot(cols_cat[blk], vectors, preferred_element_type=F32))
                partial[c, first + d] = product.reshape(SIDE, SIDE, PACK, COLS)
            where = pl.ds(begin, size)
            for by in range(1, SIDE):
                copies.start(
                    group, first_slots[g], partial.at[c, where, :, lax.rem(ypos + by, SIDE), 0:HALF],
                    recv_first.at[c, 0, by - 1, where], along_y(by),
                )
                copies.start(
                    group, first_slots[g], partial.at[c, where, lax.rem(xpos + by, SIDE), :, HALF:PACK],
                    recv_first.at[c, 1, by - 1, where], along_x(by),
                )
        yield
        for g, (begin, size) in enumerate(groups):
            where = pl.ds(begin, size)
            copies.arrived(first_slots[g], recv_first.at[c, :, :, where], sibling)
            for b in range(begin, begin + size):
                upper = partial[c, b, :, ypos, 0:HALF]
                lower = partial[c, b, xpos, :, HALF:PACK]
                for by in range(SIDE - 1):
                    upper = upper + recv_first[c, 0, by, b]
                    lower = lower + recv_first[c, 1, by, b]
                reduced[c, 0, b] = upper
                reduced[c, 1, b] = lower
            for by in range(1, SIDE):
                copies.start(
                    group, second_slots[g], reduced.at[c, 0, where, lax.rem(xpos + by, SIDE)],
                    recv_second.at[c, by - 1, where, 0:HALF], along_x(by),
                )
                copies.start(
                    group, second_slots[g], reduced.at[c, 1, where, lax.rem(ypos + by, SIDE)],
                    recv_second.at[c, by - 1, where, HALF:PACK], along_y(by),
                )
        yield
        for g, (begin, size) in enumerate(groups):
            if g:
                yield
            where = pl.ds(begin, size)
            copies.arrived(second_slots[g], recv_second.at[c, :, where], sibling)
            for b in range(begin, begin + size):
                total = jnp.concatenate([reduced[c, 0, b, xpos], reduced[c, 1, b, ypos]], 0)
                for by in range(SIDE - 1):
                    total = total + recv_second[c, by, b]
                if b == first:
                    own = total
                else:
                    recv_cube[c, 0, b] = total
                    copies.start(group, z_slot, recv_cube.at[c, 0, b], recv_cube.at[c, 1, b], along_z(b - first, members))
        if members > 1:
            copies.arrived(z_slot, recv_cube.at[c, 1, pl.ds(first + 1, members - 1)], sibling)
            for by in range(1, members):
                own = own + recv_cube[c, 1, first + by]
        return own

    def all_of(*steps):
        def run():
            for step, *which in steps:
                step(*which)

        return run

    def chain(c):
        def when_first(*steps):
            return all_of(*steps) if c == 0 else None

        solved_leaf = yield from gather_product(
            c, 0, packed(sides[0, 0], c), when_first((halve, 0, None),),
            when_first((halve, 1, pmid), (fill_rows, 0), (halve, 2, None)),
        )
        update_mid = yield from gather_product(
            c, 1, solved_leaf, when_first((fill_rows, 1),), when_first((halve, 3, ptop), (fill_rows, 2))
        )
        solved_mid = yield from gather_product(
            c, 2, packed(sides[1, 0], c) - update_mid, None, when_first((halve, 4, None), (fill_rows, 3))
        )
        update_top = yield from gather_product(
            c, 3, solved_mid, None, when_first((fill_rows, 4), (fill_cols, 0), (fill_cols, 1), (fill_cols, 2))
        )
        solved_top = yield from gather_product(
            c, 4, packed(sides[2, 0], c) - update_top, None, when_first((fill_cols, 4), (fill_cols, 3))
        )
        result[c, 2] = yield from spread_product(c, 4, solved_top)
        carry_mid = yield from spread_product(c, 3, result[c, 2])
        result[c, 1] = yield from spread_product(c, 2, solved_mid - carry_mid)
        carry_leaf = yield from spread_product(c, 1, result[c, 1])
        result[c, 0] = yield from spread_product(c, 0, solved_leaf - carry_leaf)

    chains = [chain(c) for c in range(CHAINS)]
    for _ in range(LAG):
        next(chains[0])
    done = object()
    while chains:
        chains = [one for one in reversed(chains) if next(one, done) is not done][::-1]
    for level in range(3):
        out[level, 0] = unpacked(result[0, level], result[1, level])
    copies.all_sent(SENDS - 1, sibling_half, sibling)
    for c in range(CHAINS):
        for k in range(5):
            where = pl.ds(FIRST[k], COUNT[k])
            copies.all_sent(c * 10 + k, gathered.at[c, where], sibling)
            copies.all_sent(c * 10 + 5 + k, partial.at[c, where], sibling)


def local(right_sides, inverse_leaf, inverse_mid, inverse_top, coupling_mid, coupling_top, pattern_mid, pattern_top):
    vmem = pl.BlockSpec(memory_space=pltpu.VMEM)
    smem = pl.BlockSpec(memory_space=pltpu.SMEM)
    hbm = pl.BlockSpec(memory_space=pl.ANY)
    return pl.pallas_call(
        kernel,
        out_shape=jax.ShapeDtypeStruct(right_sides.shape, F32),
        in_specs=[vmem, hbm, hbm, hbm, hbm, hbm, smem, smem],
        out_specs=vmem,
        scratch_shapes=[
            *[pltpu.VMEM((ROWS, 2 * BLOCK * count), F32) for count in COUNT],
            pltpu.VMEM((2, BLOCKS, ROWS, BLOCK), F32),
            pltpu.VMEM((BLOCKS, ROWS, BLOCK), F32),
            pltpu.VMEM((BLOCKS, 4 * ROWS, BLOCK), BF16),
            pltpu.VMEM((BLOCKS, BLOCK, 4 * ROWS), BF16),
            pltpu.VMEM((CHAINS, BLOCKS, SIDE, SIDE, PACK, COLS), F32),
            pltpu.VMEM((CHAINS, BLOCKS, SIDE, SIDE, PACK, COLS), F32),
            pltpu.VMEM((CHAINS, 2, SIDE - 1, BLOCKS, SIDE, HALF, COLS), F32),
            pltpu.VMEM((CHAINS, SIDE - 1, BLOCKS, PACK, COLS), F32),
            pltpu.VMEM((CHAINS, 2, BLOCKS, SIDE, HALF, COLS), F32),
            pltpu.VMEM((CHAINS, 2, BLOCKS, PACK, COLS), F32),
            pltpu.VMEM((CHAINS, 5, 2, PACK, COLS), F32),
            pltpu.VMEM((CHAINS, 5, 2, PACK, COLS), F32),
            pltpu.VMEM((CHAINS, 3, PACK, COLS), F32),
            pltpu.SemaphoreType.DMA((5,)),
            pltpu.SemaphoreType.DMA((SENDS,)),
            pltpu.SemaphoreType.DMA((RECEIVE,)),
        ],
        compiler_params=pltpu.CompilerParams(
            collective_id=0, has_side_effects=True, vmem_limit_bytes=62 * 2**20
        ),
        name="solve",
    )(right_sides, inverse_leaf, inverse_mid, inverse_top, coupling_mid, coupling_top, pattern_mid, pattern_top)


def solution(mesh):
    split_rows = P("cube", "front", None)
    levels = P(None, "cube", "front", None)
    return jax.shard_map(
        local, mesh=mesh, in_specs=(levels,) + (split_rows,) * 7, out_specs=levels, check_vma=False,
    )
```

```python
import functools

import jax
import jax.numpy as jnp
from jax import lax
from jax.experimental import pallas as pl
from jax.experimental.pallas import tpu as pltpu
from jax.sharding import PartitionSpec as P

MESH = pl.DeviceIdType.MESH
SIDE = 4
ROWS = 64
COLS = 128
CHAINS = 2
PACK = ROWS // CHAINS
HALF = PACK // 2
BLOCK = SIDE * SIDE * ROWS
FIRST = (0, 1, 3, 5, 9)
COUNT = (1, 2, 2, 4, 4)
BLOCKS = 13
TURNS = ((1, 3), (2,))
LAG = 1
F32, BF16 = jnp.float32, jnp.bfloat16


def split(values):
    high = values.astype(BF16)
    low = (values - high.astype(F32)).astype(BF16)
    return high, low


def left_lanes(values):
    return lax.broadcasted_iota(jnp.int32, values.shape, values.ndim - 1) < COLS // 2


def side_by_side(packed):
    flat = packed.reshape(-1, COLS)
    turned = pltpu.roll(flat, COLS // 2, 1)
    left = left_lanes(flat)
    high, low = flat.astype(BF16).astype(F32), turned - turned.astype(BF16).astype(F32)
    upper = jnp.where(left, high, low).astype(BF16)
    high, low = turned.astype(BF16).astype(F32), flat - flat.astype(BF16).astype(F32)
    lower = jnp.where(left, high, low).astype(BF16)
    both = jnp.concatenate([upper.reshape(packed.shape), lower.reshape(packed.shape)], 1)
    return both.reshape(-1, COLS)


def packed_sum(product):
    total = (product + pltpu.roll(product, COLS // 2, 1)).reshape(-1, ROWS, COLS)
    upper, lower = total[:, :PACK], total[:, PACK:]
    return jnp.where(left_lanes(upper), upper, lower)


def packed(values, chain):
    upper, lower = values[:PACK], values[PACK:]
    if chain == 0:
        return jnp.where(left_lanes(upper), upper, pltpu.roll(lower, COLS // 2, 1))
    return jnp.where(left_lanes(upper), pltpu.roll(upper, COLS // 2, 1), lower)


def unpacked(first, second):
    left = left_lanes(first)
    upper = jnp.where(left, first, pltpu.roll(second, COLS // 2, 1))
    lower = jnp.where(left, pltpu.roll(first, COLS // 2, 1), second)
    return jnp.concatenate([upper, lower], 0)


class Copies:
    def __init__(self, send, recv):
        self.send, self.recv, self.used = send, recv, 0

    def slot(self):
        self.used += 1
        assert self.used <= RECEIVE
        return self.used - 1

    def start(self, group, slot, src, dst, device):
        pltpu.make_async_remote_copy(
            src_ref=src, dst_ref=dst, send_sem=self.send.at[group], recv_sem=self.recv.at[slot],
            device_id=device, device_id_type=MESH,
        ).start()

    def arrived(self, slot, dst, device):
        pltpu.make_async_remote_copy(
            src_ref=dst, dst_ref=dst, send_sem=self.send.at[0], recv_sem=self.recv.at[slot],
            device_id=device, device_id_type=MESH,
        ).wait_recv()

    def all_sent(self, group, as_many, device):
        pltpu.make_async_remote_copy(
            src_ref=as_many, dst_ref=as_many, send_sem=self.send.at[group], recv_sem=self.recv.at[0],
            device_id=device, device_id_type=MESH,
        ).wait_send()


SENDS = CHAINS * 10 + 1
RECEIVE = 131


def kernel(
    sides, leaf, mid, top, cmid, ctop, pmid, ptop, out,
    raw_leaf, raw_cmid, raw_mid, raw_ctop, raw_top, halves, sibling_half, rows_cat, cols_cat,
    gathered, partial, recv_first, recv_second, reduced, recv_cube, mine, cross, result, local_sem, send, recv,
):
    cube = lax.axis_index("cube")
    front = lax.axis_index("front")
    core = lax.rem(front, 2)
    ypos = lax.rem(front // 2, SIDE)
    xpos = front // (2 * SIDE)

    def at(x, y, z, c):
        return (z, (x * SIDE + y) * 2 + c)

    def along_x(by):
        return at(lax.rem(xpos + by, SIDE), ypos, cube, core)

    def along_y(by):
        return at(xpos, lax.rem(ypos + by, SIDE), cube, core)

    def along_z(by, members):
        member = lax.rem(cube, members)
        return at(xpos, ypos, cube - member + lax.rem(member + by, members), core)

    sibling = at(xpos, ypos, cube, 1 - core)
    copies = Copies(send, recv)

    raws = (raw_leaf, raw_cmid, raw_mid, raw_ctop, raw_top)
    loads = []
    for k, (src, dst) in enumerate(zip((leaf, cmid, mid, ctop, top), raws)):
        load = pltpu.make_async_copy(src.at[0], dst, local_sem.at[k])
        load.start()
        loads.append(load)

    barrier = pltpu.get_barrier_semaphore()
    peers = [sibling]
    for by in range(1, SIDE):
        peers += [along_x(by), along_y(by), along_z(by, 4)]
    for peer in peers:
        pl.semaphore_signal(barrier, inc=1, device_id=peer, device_id_type=MESH)
    pl.semaphore_wait(barrier, len(peers))

    lane = lax.broadcasted_iota(jnp.int32, (ROWS, 128), 1)
    first_half = lane < ROWS

    half_slots = {}

    def halve(k, pattern):
        loads[k].wait()

        def one(m, carry):
            for i in range(BLOCK // 128):
                at_column = pl.multiple_of(m * (2 * BLOCK) + i * 256, 256)
                left = raws[k][:, pl.ds(at_column, 128)]
                right = raws[k][:, pl.ds(at_column + 128, 128)]
                low = jnp.where(first_half, left, pltpu.roll(right, ROWS, 1))
                high = jnp.where(first_half, pltpu.roll(left, ROWS, 1), right)
                if pattern is not None:
                    tile = m * (2 * BLOCK // ROWS) + 4 * i
                    keep = [pattern[0, 0, tile + j].astype(F32) for j in range(4)]
                    low = low * jnp.where(first_half, keep[0], keep[2])
                    high = high * jnp.where(first_half, keep[1], keep[3])
                halves[0, FIRST[k] + m, :, i * 128 : (i + 1) * 128] = low
                halves[1, FIRST[k] + m, :, i * 128 : (i + 1) * 128] = high
            return carry

        lax.fori_loop(0, COUNT[k], one, 0)
        where = pl.ds(FIRST[k], COUNT[k])
        half_slots[k] = copies.slot()
        copies.start(SENDS - 1, half_slots[k], halves.at[1 - core, where], sibling_half.at[where], sibling)

    def fill_rows(k):
        copies.arrived(half_slots[k], sibling_half.at[pl.ds(FIRST[k], COUNT[k])], sibling)

        def one(m, carry):
            blk = FIRST[k] + m
            for first, source in ((0, halves[core, blk]), (2 * ROWS, sibling_half[blk])):
                high, low = split(source)
                rows_cat[blk, first : first + ROWS] = high
                rows_cat[blk, first + ROWS : first + 2 * ROWS] = low
            return carry

        lax.fori_loop(0, COUNT[k], one, 0)

    def fill_cols(k):
        def one(m, carry):
            blk = FIRST[k] + m
            for i in range(BLOCK // 128):
                part = slice(i * 128, (i + 1) * 128)
                both = jnp.concatenate([halves[core, blk, :, part], sibling_half[blk, :, part]], 0)
                high, low = split(both.T)
                cols_cat[blk, part, :128] = high
                cols_cat[blk, part, 128:] = low
            return carry

        lax.fori_loop(0, COUNT[k], one, 0)

    def gather_product(c, k, shard, early=None, late=None):
        first, members = FIRST[k], COUNT[k]
        member = lax.rem(cube, members)
        group = c * 10 + k
        gathered[c, first, xpos, ypos] = shard
        groups = [(first, 1)] + ([(first + 1, members - 1)] if members > 1 else [])
        z_slot = copies.slot() if members > 1 else None
        for by in range(1, members):
            copies.start(
                group, z_slot, gathered.at[c, first, xpos, ypos],
                gathered.at[c, first + members - by, xpos, ypos], along_z(by, members),
            )
        ring_slots = [[copies.slot() for _ in TURNS] for _ in groups]
        next_slots = [copies.slot() for _ in groups]

        def to_rings(g):
            where = pl.ds(*groups[g])
            block = gathered.at[c, where, xpos, ypos]
            for slot, turn in zip(ring_slots[g], TURNS):
                for by in turn:
                    copies.start(group, slot, block, block, along_x(by))
                    copies.start(group, slot, block, block, along_y(by))

        def onward(g):
            where = pl.ds(*groups[g])
            for slot, turn in zip(ring_slots[g], TURNS):
                copies.arrived(slot, gathered.at[c, where, 0 : 2 * len(turn), ypos], sibling)
                for by in turn:
                    x_from, y_from = lax.rem(xpos + SIDE - by, SIDE), lax.rem(ypos + SIDE - by, SIDE)
                    block_x = gathered.at[c, where, x_from, ypos, 0:HALF]
                    block_y = gathered.at[c, where, xpos, y_from, HALF:PACK]
                    for on in (1, 3, 2):
                        copies.start(group, next_slots[g], block_x, block_x, along_y(on))
                        copies.start(group, next_slots[g], block_y, block_y, along_x(on))

        def multiply(d, rows):
            vectors = side_by_side(gathered[c, first + d].reshape(SIDE * SIDE, PACK, COLS))
            blk = first + lax.rem(member + d, members)
            return jnp.dot(rows_cat[blk, rows], vectors, preferred_element_type=F32)

        to_rings(0)
        if early:
            early()
        yield
        if members > 1:
            copies.arrived(z_slot, gathered.at[c, pl.ds(first + 1, members - 1), xpos, ypos], sibling)
            to_rings(1)
            onward(0)
            yield
        onward(len(groups) - 1)
        if late:
            late()
        yield
        own, other = slice(0, 2 * ROWS), slice(2 * ROWS, 4 * ROWS)
        total = jnp.zeros((4 * ROWS, COLS), F32)
        for g, (begin, size) in enumerate(groups):
            copies.arrived(next_slots[g], gathered.at[c, pl.ds(begin, size), 0 : SIDE - 1, 0 : SIDE - 1], sibling)
            for d in range(begin - first, begin - first + size):
                if d < members - 1:
                    total = total + multiply(d, slice(0, 4 * ROWS))

        def last(rows):
            part = total[rows] + multiply(members - 1, rows)
            return packed_sum(part[:ROWS] + part[ROWS:])[0]

        cross[c, k, 0] = last(other)
        slot = copies.slot()
        copies.start(group, slot, cross.at[c, k, 0], cross.at[c, k, 1], sibling)
        mine_now = last(own)
        copies.arrived(slot, cross.at[c, k, 1], sibling)
        return mine_now + cross[c, k, 1]

    def spread_product(c, k, shard):
        first, members = FIRST[k], COUNT[k]
        member = lax.rem(cube, members)
        group = c * 10 + 5 + k
        mine[c, k, 0] = shard
        slot = copies.slot()
        copies.start(group, slot, mine.at[c, k, 0], mine.at[c, k, 1], sibling)
        groups = ([(first + 1, members - 1)] if members > 1 else []) + [(first, 1)]
        first_slots = [copies.slot() for _ in groups]
        second_slots = [copies.slot() for _ in groups]
        z_slot = copies.slot() if members > 1 else None
        copies.arrived(slot, mine.at[c, k, 1], sibling)
        vectors = side_by_side(mine[c, k])
        vectors = jnp.concatenate([vectors, vectors], 0)
        for g, (begin, size) in enumerate(groups):
            for d in range(begin - first, begin - first + size):
                blk = first + lax.rem(member + d, members)
                product = packed_sum(jnp.dot(cols_cat[blk], vectors, preferred_element_type=F32))
                partial[c, first + d] = product.reshape(SIDE, SIDE, PACK, COLS)
            where = pl.ds(begin, size)
            for by in range(1, SIDE):
                copies.start(
                    group, first_slots[g], partial.at[c, where, :, lax.rem(ypos + by, SIDE), 0:HALF],
                    recv_first.at[c, 0, by - 1, where], along_y(by),
                )
                copies.start(
                    group, first_slots[g], partial.at[c, where, lax.rem(xpos + by, SIDE), :, HALF:PACK],
                    recv_first.at[c, 1, by - 1, where], along_x(by),
                )
        yield
        for g, (begin, size) in enumerate(groups):
            where = pl.ds(begin, size)
            copies.arrived(first_slots[g], recv_first.at[c, :, :, where], sibling)
            for b in range(begin, begin + size):
                upper = partial[c, b, :, ypos, 0:HALF]
                lower = partial[c, b, xpos, :, HALF:PACK]
                for by in range(SIDE - 1):
                    upper = upper + recv_first[c, 0, by, b]
                    lower = lower + recv_first[c, 1, by, b]
                reduced[c, 0, b] = upper
                reduced[c, 1, b] = lower
            for by in range(1, SIDE):
                copies.start(
                    group, second_slots[g], reduced.at[c, 0, where, lax.rem(xpos + by, SIDE)],
                    recv_second.at[c, by - 1, where, 0:HALF], along_x(by),
                )
                copies.start(
                    group, second_slots[g], reduced.at[c, 1, where, lax.rem(ypos + by, SIDE)],
                    recv_second.at[c, by - 1, where, HALF:PACK], along_y(by),
                )
        yield
        for g, (begin, size) in enumerate(groups):
            if g:
                yield
            where = pl.ds(begin, size)
            copies.arrived(second_slots[g], recv_second.at[c, :, where], sibling)
            for b in range(begin, begin + size):
                total = jnp.concatenate([reduced[c, 0, b, xpos], reduced[c, 1, b, ypos]], 0)
                for by in range(SIDE - 1):
                    total = total + recv_second[c, by, b]
                if b == first:
                    own = total
                else:
                    recv_cube[c, 0, b] = total
                    copies.start(group, z_slot, recv_cube.at[c, 0, b], recv_cube.at[c, 1, b], along_z(b - first, members))
        if members > 1:
            copies.arrived(z_slot, recv_cube.at[c, 1, pl.ds(first + 1, members - 1)], sibling)
            for by in range(1, members):
                own = own + recv_cube[c, 1, first + by]
        return own

    def all_of(*steps):
        def run():
            for step, *which in steps:
                step(*which)

        return run

    def chain(c):
        def when_first(*steps):
            return all_of(*steps) if c == 0 else None

        solved_leaf = yield from gather_product(
            c, 0, packed(sides[0, 0], c), when_first((halve, 0, None),),
            when_first((halve, 1, pmid), (fill_rows, 0), (halve, 2, None)),
        )
        update_mid = yield from gather_product(
            c, 1, solved_leaf, when_first((fill_rows, 1),), when_first((halve, 3, ptop), (fill_rows, 2))
        )
        solved_mid = yield from gather_product(
            c, 2, packed(sides[1, 0], c) - update_mid, None, when_first((halve, 4, None), (fill_rows, 3))
        )
        update_top = yield from gather_product(
            c, 3, solved_mid, None, when_first((fill_rows, 4), (fill_cols, 0), (fill_cols, 1), (fill_cols, 2))
        )
        solved_top = yield from gather_product(
            c, 4, packed(sides[2, 0], c) - update_top, None, when_first((fill_cols, 4), (fill_cols, 3))
        )
        result[c, 2] = yield from spread_product(c, 4, solved_top)
        carry_mid = yield from spread_product(c, 3, result[c, 2])
        result[c, 1] = yield from spread_product(c, 2, solved_mid - carry_mid)
        carry_leaf = yield from spread_product(c, 1, result[c, 1])
        result[c, 0] = yield from spread_product(c, 0, solved_leaf - carry_leaf)

    chains = [chain(c) for c in range(CHAINS)]
    for _ in range(LAG):
        next(chains[0])
    done = object()
    while chains:
        chains = [one for one in reversed(chains) if next(one, done) is not done][::-1]
    for level in range(3):
        out[level, 0] = unpacked(result[0, level], result[1, level])
    copies.all_sent(SENDS - 1, sibling_half, sibling)
    for c in range(CHAINS):
        for k in range(5):
            where = pl.ds(FIRST[k], COUNT[k])
            copies.all_sent(c * 10 + k, gathered.at[c, where], sibling)
            copies.all_sent(c * 10 + 5 + k, partial.at[c, where], sibling)


def local(right_sides, inverse_leaf, inverse_mid, inverse_top, coupling_mid, coupling_top, pattern_mid, pattern_top):
    vmem = pl.BlockSpec(memory_space=pltpu.VMEM)
    smem = pl.BlockSpec(memory_space=pltpu.SMEM)
    hbm = pl.BlockSpec(memory_space=pl.ANY)
    return pl.pallas_call(
        kernel,
        out_shape=jax.ShapeDtypeStruct(right_sides.shape, F32),
        in_specs=[vmem, hbm, hbm, hbm, hbm, hbm, smem, smem],
        out_specs=vmem,
        scratch_shapes=[
            *[pltpu.VMEM((ROWS, 2 * BLOCK * count), F32) for count in COUNT],
            pltpu.VMEM((2, BLOCKS, ROWS, BLOCK), F32),
            pltpu.VMEM((BLOCKS, ROWS, BLOCK), F32),
            pltpu.VMEM((BLOCKS, 4 * ROWS, BLOCK), BF16),
            pltpu.VMEM((BLOCKS, BLOCK, 4 * ROWS), BF16),
            pltpu.VMEM((CHAINS, BLOCKS, SIDE, SIDE, PACK, COLS), F32),
            pltpu.VMEM((CHAINS, BLOCKS, SIDE, SIDE, PACK, COLS), F32),
            pltpu.VMEM((CHAINS, 2, SIDE - 1, BLOCKS, SIDE, HALF, COLS), F32),
            pltpu.VMEM((CHAINS, SIDE - 1, BLOCKS, PACK, COLS), F32),
            pltpu.VMEM((CHAINS, 2, BLOCKS, SIDE, HALF, COLS), F32),
            pltpu.VMEM((CHAINS, 2, BLOCKS, PACK, COLS), F32),
            pltpu.VMEM((CHAINS, 5, 2, PACK, COLS), F32),
            pltpu.VMEM((CHAINS, 5, 2, PACK, COLS), F32),
            pltpu.VMEM((CHAINS, 3, PACK, COLS), F32),
            pltpu.SemaphoreType.DMA((5,)),
            pltpu.SemaphoreType.DMA((SENDS,)),
            pltpu.SemaphoreType.DMA((RECEIVE,)),
        ],
        compiler_params=pltpu.CompilerParams(
            collective_id=0, has_side_effects=True, vmem_limit_bytes=62 * 2**20
        ),
        name="solve",
    )(right_sides, inverse_leaf, inverse_mid, inverse_top, coupling_mid, coupling_top, pattern_mid, pattern_top)


def solution(mesh):
    split_rows = P("cube", "front", None)
    levels = P(None, "cube", "front", None)
    return jax.shard_map(
        local, mesh=mesh, in_specs=(levels,) + (split_rows,) * 7, out_specs=levels, check_vma=False,
    )
```

```python
import functools

import jax
import jax.numpy as jnp
from jax import lax
from jax.experimental import pallas as pl
from jax.experimental.pallas import tpu as pltpu
from jax.sharding import PartitionSpec as P

MESH = pl.DeviceIdType.MESH
SIDE = 4
ROWS = 64
COLS = 128
CHAINS = 2
PACK = ROWS // CHAINS
HALF = PACK // 2
BLOCK = SIDE * SIDE * ROWS
FIRST = (0, 1, 3, 5, 9)
COUNT = (1, 2, 2, 4, 4)
BLOCKS = 13
TURNS = ((1, 3), (2,))
LAG = 1
F32, BF16 = jnp.float32, jnp.bfloat16


def split(values):
    high = values.astype(BF16)
    low = (values - high.astype(F32)).astype(BF16)
    return high, low


def left_lanes(values):
    return lax.broadcasted_iota(jnp.int32, values.shape, values.ndim - 1) < COLS // 2


def side_by_side(packed):
    flat = packed.reshape(-1, COLS)
    turned = pltpu.roll(flat, COLS // 2, 1)
    left = left_lanes(flat)
    high, low = flat.astype(BF16).astype(F32), turned - turned.astype(BF16).astype(F32)
    upper = jnp.where(left, high, low).astype(BF16)
    high, low = turned.astype(BF16).astype(F32), flat - flat.astype(BF16).astype(F32)
    lower = jnp.where(left, high, low).astype(BF16)
    both = jnp.concatenate([upper.reshape(packed.shape), lower.reshape(packed.shape)], 1)
    return both.reshape(-1, COLS)


def packed_sum(product):
    total = (product + pltpu.roll(product, COLS // 2, 1)).reshape(-1, ROWS, COLS)
    upper, lower = total[:, :PACK], total[:, PACK:]
    return jnp.where(left_lanes(upper), upper, lower)


def packed(values, chain):
    upper, lower = values[:PACK], values[PACK:]
    if chain == 0:
        return jnp.where(left_lanes(upper), upper, pltpu.roll(lower, COLS // 2, 1))
    return jnp.where(left_lanes(upper), pltpu.roll(upper, COLS // 2, 1), lower)


def unpacked(first, second):
    left = left_lanes(first)
    upper = jnp.where(left, first, pltpu.roll(second, COLS // 2, 1))
    lower = jnp.where(left, pltpu.roll(first, COLS // 2, 1), second)
    return jnp.concatenate([upper, lower], 0)


class Copies:
    def __init__(self, send, recv):
        self.send, self.recv, self.used = send, recv, 0

    def slot(self):
        self.used += 1
        assert self.used <= RECEIVE
        return self.used - 1

    def start(self, group, slot, src, dst, device):
        pltpu.make_async_remote_copy(
            src_ref=src, dst_ref=dst, send_sem=self.send.at[group], recv_sem=self.recv.at[slot],
            device_id=device, device_id_type=MESH,
        ).start()

    def arrived(self, slot, dst, device):
        pltpu.make_async_remote_copy(
            src_ref=dst, dst_ref=dst, send_sem=self.send.at[0], recv_sem=self.recv.at[slot],
            device_id=device, device_id_type=MESH,
        ).wait_recv()

    def all_sent(self, group, as_many, device):
        pltpu.make_async_remote_copy(
            src_ref=as_many, dst_ref=as_many, send_sem=self.send.at[group], recv_sem=self.recv.at[0],
            device_id=device, device_id_type=MESH,
        ).wait_send()


SENDS = CHAINS * 10 + 1
RECEIVE = 131


def kernel(
    sides, leaf, mid, top, cmid, ctop, pmid, ptop, out,
    raw_leaf, raw_cmid, raw_mid, raw_ctop, raw_top, halves, sibling_half, rows_cat, cols_cat,
    gathered, partial, recv_first, recv_second, reduced, recv_cube, mine, cross, result, local_sem, send, recv,
):
    cube = lax.axis_index("cube")
    front = lax.axis_index("front")
    core = lax.rem(front, 2)
    ypos = lax.rem(front // 2, SIDE)
    xpos = front // (2 * SIDE)

    def at(x, y, z, c):
        return (z, (x * SIDE + y) * 2 + c)

    def along_x(by):
        return at(lax.rem(xpos + by, SIDE), ypos, cube, core)

    def along_y(by):
        return at(xpos, lax.rem(ypos + by, SIDE), cube, core)

    def along_z(by, members):
        member = lax.rem(cube, members)
        return at(xpos, ypos, cube - member + lax.rem(member + by, members), core)

    sibling = at(xpos, ypos, cube, 1 - core)
    copies = Copies(send, recv)

    raws = (raw_leaf, raw_cmid, raw_mid, raw_ctop, raw_top)
    loads = []
    for k, (src, dst) in enumerate(zip((leaf, cmid, mid, ctop, top), raws)):
        load = pltpu.make_async_copy(src.at[0], dst, local_sem.at[k])
        load.start()
        loads.append(load)

    barrier = pltpu.get_barrier_semaphore()
    peers = [sibling]
    for by in range(1, SIDE):
        peers += [along_x(by), along_y(by), along_z(by, 4)]
    for peer in peers:
        pl.semaphore_signal(barrier, inc=1, device_id=peer, device_id_type=MESH)
    pl.semaphore_wait(barrier, len(peers))

    lane = lax.broadcasted_iota(jnp.int32, (ROWS, 128), 1)
    first_half = lane < ROWS

    half_slots = {}

    def halve(k, pattern):
        loads[k].wait()

        def one(m, carry):
            for i in range(BLOCK // 128):
                at_column = pl.multiple_of(m * (2 * BLOCK) + i * 256, 256)
                left = raws[k][:, pl.ds(at_column, 128)]
                right = raws[k][:, pl.ds(at_column + 128, 128)]
                low = jnp.where(first_half, left, pltpu.roll(right, ROWS, 1))
                high = jnp.where(first_half, pltpu.roll(left, ROWS, 1), right)
                if pattern is not None:
                    tile = m * (2 * BLOCK // ROWS) + 4 * i
                    keep = [pattern[0, 0, tile + j].astype(F32) for j in range(4)]
                    low = low * jnp.where(first_half, keep[0], keep[2])
                    high = high * jnp.where(first_half, keep[1], keep[3])
                halves[0, FIRST[k] + m, :, i * 128 : (i + 1) * 128] = low
                halves[1, FIRST[k] + m, :, i * 128 : (i + 1) * 128] = high
            return carry

        lax.fori_loop(0, COUNT[k], one, 0)
        where = pl.ds(FIRST[k], COUNT[k])
        half_slots[k] = copies.slot()
        copies.start(SENDS - 1, half_slots[k], halves.at[1 - core, where], sibling_half.at[where], sibling)

    def fill_rows(k):
        copies.arrived(half_slots[k], sibling_half.at[pl.ds(FIRST[k], COUNT[k])], sibling)

        def one(m, carry):
            blk = FIRST[k] + m
            for first, source in ((0, halves[core, blk]), (ROWS, sibling_half[blk])):
                high, low = split(source)
                rows_cat[blk, first : first + ROWS] = high
                rows_cat[blk, 2 * ROWS + first : 3 * ROWS + first] = low
            return carry

        lax.fori_loop(0, COUNT[k], one, 0)

    def fill_cols(k):
        def one(m, carry):
            blk = FIRST[k] + m
            for i in range(BLOCK // 128):
                part = slice(i * 128, (i + 1) * 128)
                both = jnp.concatenate([halves[core, blk, :, part], sibling_half[blk, :, part]], 0)
                high, low = split(both.T)
                cols_cat[blk, part, :128] = high
                cols_cat[blk, part, 128:] = low
            return carry

        lax.fori_loop(0, COUNT[k], one, 0)

    def gather_product(c, k, shard, early=None, late=None, beside=None):
        first, members = FIRST[k], COUNT[k]
        member = lax.rem(cube, members)
        group = c * 10 + k
        gathered[c, first, xpos, ypos] = shard
        groups = [(first, 1)] + ([(first + 1, members - 1)] if members > 1 else [])
        z_slot = copies.slot() if members > 1 else None
        for by in range(1, members):
            copies.start(
                group, z_slot, gathered.at[c, first, xpos, ypos],
                gathered.at[c, first + members - by, xpos, ypos], along_z(by, members),
            )
        ring_slots = [[copies.slot() for _ in TURNS] for _ in groups]
        next_slots = [copies.slot() for _ in groups]

        def to_rings(g):
            where = pl.ds(*groups[g])
            block = gathered.at[c, where, xpos, ypos]
            for slot, turn in zip(ring_slots[g], TURNS):
                for by in turn:
                    copies.start(group, slot, block, block, along_x(by))
                    copies.start(group, slot, block, block, along_y(by))

        def onward(g):
            where = pl.ds(*groups[g])
            for slot, turn in zip(ring_slots[g], TURNS):
                copies.arrived(slot, gathered.at[c, where, 0 : 2 * len(turn), ypos], sibling)
                for by in turn:
                    x_from, y_from = lax.rem(xpos + SIDE - by, SIDE), lax.rem(ypos + SIDE - by, SIDE)
                    block_x = gathered.at[c, where, x_from, ypos, 0:HALF]
                    block_y = gathered.at[c, where, xpos, y_from, HALF:PACK]
                    for on in (1, 3, 2):
                        copies.start(group, next_slots[g], block_x, block_x, along_y(on))
                        copies.start(group, next_slots[g], block_y, block_y, along_x(on))

        def multiply(d):
            vectors = side_by_side(gathered[c, first + d].reshape(SIDE * SIDE, PACK, COLS))
            blk = first + lax.rem(member + d, members)
            return jnp.dot(rows_cat[blk], vectors, preferred_element_type=F32)

        to_rings(0)
        if early:
            early()
        yield
        if members > 1:
            copies.arrived(z_slot, gathered.at[c, pl.ds(first + 1, members - 1), xpos, ypos], sibling)
            to_rings(1)
            onward(0)
            yield
        onward(len(groups) - 1)
        if late:
            late()
        yield
        total = None
        for g, (begin, size) in enumerate(groups):
            copies.arrived(next_slots[g], gathered.at[c, pl.ds(begin, size), 0 : SIDE - 1, 0 : SIDE - 1], sibling)
            for d in range(begin - first, begin - first + size):
                term = multiply(d)
                total = term if total is None else total + term
        total = packed_sum(total[: 2 * ROWS] + total[2 * ROWS :])
        cross[c, k, 0] = total[1]
        slot = copies.slot()
        copies.start(group, slot, cross.at[c, k, 0], cross.at[c, k, 1], sibling)
        if beside:
            beside()
        copies.arrived(slot, cross.at[c, k, 1], sibling)
        return total[0] + cross[c, k, 1]

    def spread_product(c, k, shard):
        first, members = FIRST[k], COUNT[k]
        member = lax.rem(cube, members)
        group = c * 10 + 5 + k
        mine[c, k, 0] = shard
        slot = copies.slot()
        copies.start(group, slot, mine.at[c, k, 0], mine.at[c, k, 1], sibling)
        groups = ([(first + 1, members - 1)] if members > 1 else []) + [(first, 1)]
        first_slots = [copies.slot() for _ in groups]
        second_slots = [copies.slot() for _ in groups]
        z_slot = copies.slot() if members > 1 else None
        copies.arrived(slot, mine.at[c, k, 1], sibling)
        vectors = side_by_side(mine[c, k])
        vectors = jnp.concatenate([vectors, vectors], 0)
        for g, (begin, size) in enumerate(groups):
            for d in range(begin - first, begin - first + size):
                blk = first + lax.rem(member + d, members)
                product = packed_sum(jnp.dot(cols_cat[blk], vectors, preferred_element_type=F32))
                partial[c, first + d] = product.reshape(SIDE, SIDE, PACK, COLS)
            where = pl.ds(begin, size)
            for by in range(1, SIDE):
                copies.start(
                    group, first_slots[g], partial.at[c, where, :, lax.rem(ypos + by, SIDE), 0:HALF],
                    recv_first.at[c, 0, by - 1, where], along_y(by),
                )
                copies.start(
                    group, first_slots[g], partial.at[c, where, lax.rem(xpos + by, SIDE), :, HALF:PACK],
                    recv_first.at[c, 1, by - 1, where], along_x(by),
                )
        yield
        for g, (begin, size) in enumerate(groups):
            where = pl.ds(begin, size)
            copies.arrived(first_slots[g], recv_first.at[c, :, :, where], sibling)
            for b in range(begin, begin + size):
                upper = partial[c, b, :, ypos, 0:HALF]
                lower = partial[c, b, xpos, :, HALF:PACK]
                for by in range(SIDE - 1):
                    upper = upper + recv_first[c, 0, by, b]
                    lower = lower + recv_first[c, 1, by, b]
                reduced[c, 0, b] = upper
                reduced[c, 1, b] = lower
            for by in range(1, SIDE):
                copies.start(
                    group, second_slots[g], reduced.at[c, 0, where, lax.rem(xpos + by, SIDE)],
                    recv_second.at[c, by - 1, where, 0:HALF], along_x(by),
                )
                copies.start(
                    group, second_slots[g], reduced.at[c, 1, where, lax.rem(ypos + by, SIDE)],
                    recv_second.at[c, by - 1, where, HALF:PACK], along_y(by),
                )
        yield
        for g, (begin, size) in enumerate(groups):
            if g:
                yield
            where = pl.ds(begin, size)
            copies.arrived(second_slots[g], recv_second.at[c, :, where], sibling)
            for b in range(begin, begin + size):
                total = jnp.concatenate([reduced[c, 0, b, xpos], reduced[c, 1, b, ypos]], 0)
                for by in range(SIDE - 1):
                    total = total + recv_second[c, by, b]
                if b == first:
                    own = total
                else:
                    recv_cube[c, 0, b] = total
                    copies.start(group, z_slot, recv_cube.at[c, 0, b], recv_cube.at[c, 1, b], along_z(b - first, members))
        if members > 1:
            copies.arrived(z_slot, recv_cube.at[c, 1, pl.ds(first + 1, members - 1)], sibling)
            for by in range(1, members):
                own = own + recv_cube[c, 1, first + by]
        return own

    def all_of(*steps):
        def run():
            for step, *which in steps:
                step(*which)

        return run

    def chain(c):
        def when_first(*steps):
            return all_of(*steps) if c == 0 else None

        def beside(first_steps, second_steps):
            return all_of(*(second_steps if c else first_steps))

        solved_leaf = yield from gather_product(
            c, 0, packed(sides[0, 0], c), when_first((halve, 0, None)), when_first((halve, 1, pmid), (fill_rows, 0)),
            beside([(halve, 2, None)], [(halve, 3, ptop)]),
        )
        update_mid = yield from gather_product(
            c, 1, solved_leaf, None, when_first((fill_rows, 1)), beside([(halve, 4, None)], [(fill_rows, 2)])
        )
        solved_mid = yield from gather_product(
            c, 2, packed(sides[1, 0], c) - update_mid, None, None, beside([(fill_rows, 3)], [(fill_rows, 4)])
        )
        update_top = yield from gather_product(
            c, 3, solved_mid, None, None, beside([(fill_cols, 4)], [(fill_cols, 2), (fill_cols, 1)])
        )
        solved_top = yield from gather_product(
            c, 4, packed(sides[2, 0], c) - update_top, None, None, beside([(fill_cols, 3)], [(fill_cols, 0)])
        )
        result[c, 2] = yield from spread_product(c, 4, solved_top)
        carry_mid = yield from spread_product(c, 3, result[c, 2])
        result[c, 1] = yield from spread_product(c, 2, solved_mid - carry_mid)
        carry_leaf = yield from spread_product(c, 1, result[c, 1])
        result[c, 0] = yield from spread_product(c, 0, solved_leaf - carry_leaf)

    chains = [chain(c) for c in range(CHAINS)]
    for _ in range(LAG):
        next(chains[0])
    done = object()
    while chains:
        chains = [one for one in reversed(chains) if next(one, done) is not done][::-1]
    for level in range(3):
        out[level, 0] = unpacked(result[0, level], result[1, level])
    copies.all_sent(SENDS - 1, sibling_half, sibling)
    for c in range(CHAINS):
        for k in range(5):
            where = pl.ds(FIRST[k], COUNT[k])
            copies.all_sent(c * 10 + k, gathered.at[c, where], sibling)
            copies.all_sent(c * 10 + 5 + k, partial.at[c, where], sibling)


def local(right_sides, inverse_leaf, inverse_mid, inverse_top, coupling_mid, coupling_top, pattern_mid, pattern_top):
    vmem = pl.BlockSpec(memory_space=pltpu.VMEM)
    smem = pl.BlockSpec(memory_space=pltpu.SMEM)
    hbm = pl.BlockSpec(memory_space=pl.ANY)
    return pl.pallas_call(
        kernel,
        out_shape=jax.ShapeDtypeStruct(right_sides.shape, F32),
        in_specs=[vmem, hbm, hbm, hbm, hbm, hbm, smem, smem],
        out_specs=vmem,
        scratch_shapes=[
            *[pltpu.VMEM((ROWS, 2 * BLOCK * count), F32) for count in COUNT],
            pltpu.VMEM((2, BLOCKS, ROWS, BLOCK), F32),
            pltpu.VMEM((BLOCKS, ROWS, BLOCK), F32),
            pltpu.VMEM((BLOCKS, 4 * ROWS, BLOCK), BF16),
            pltpu.VMEM((BLOCKS, BLOCK, 4 * ROWS), BF16),
            pltpu.VMEM((CHAINS, BLOCKS, SIDE, SIDE, PACK, COLS), F32),
            pltpu.VMEM((CHAINS, BLOCKS, SIDE, SIDE, PACK, COLS), F32),
            pltpu.VMEM((CHAINS, 2, SIDE - 1, BLOCKS, SIDE, HALF, COLS), F32),
            pltpu.VMEM((CHAINS, SIDE - 1, BLOCKS, PACK, COLS), F32),
            pltpu.VMEM((CHAINS, 2, BLOCKS, SIDE, HALF, COLS), F32),
            pltpu.VMEM((CHAINS, 2, BLOCKS, PACK, COLS), F32),
            pltpu.VMEM((CHAINS, 5, 2, PACK, COLS), F32),
            pltpu.VMEM((CHAINS, 5, 2, PACK, COLS), F32),
            pltpu.VMEM((CHAINS, 3, PACK, COLS), F32),
            pltpu.SemaphoreType.DMA((5,)),
            pltpu.SemaphoreType.DMA((SENDS,)),
            pltpu.SemaphoreType.DMA((RECEIVE,)),
        ],
        compiler_params=pltpu.CompilerParams(
            collective_id=0, has_side_effects=True, vmem_limit_bytes=62 * 2**20
        ),
        name="solve",
    )(right_sides, inverse_leaf, inverse_mid, inverse_top, coupling_mid, coupling_top, pattern_mid, pattern_top)


def solution(mesh):
    split_rows = P("cube", "front", None)
    levels = P(None, "cube", "front", None)
    return jax.shard_map(
        local, mesh=mesh, in_specs=(levels,) + (split_rows,) * 7, out_specs=levels, check_vma=False,
    )
```
